32 devices in a mesh: grp: 2 (over x), sta: 16 (over z, y, core).
Axes of the slice: x: 2, y: 2, z: 4, core: 2. Of those that a mesh axis runs over, the one named last changes fastest.
Arguments:
- noise_window: float32 [1024, 4096], P(('grp', 'sta')), parts along dimension 0, may hold values from -6 to 6
- fir_taps: float32 [1024, 129], P(('grp', 'sta')), parts along dimension 0, may hold values from -0.5 to 0.5
- matchings: int32 [4, 16], replicated, may hold values from 0 to 15, each once within a row
- block_device: int32 [16], replicated, may hold values from 0 to 15, each once
Outputs:
- xcorr: float32 [4, 1024, 128], P(None, ('grp', 'sta')), parts along dimension 1
The draws below stay inside these ranges and needn't reach their ends.
There are 2 independent parts, one for each index of `grp`. The reference program is written for one: setup_inputs(seed, part) draws one part's arguments, and reference() takes and returns one part's arrays. A program takes and returns all parts, laid end to end along the dimension named above; an argument that names none is the same for every part. Nothing has to cross between parts.
Inputs may be any that keep to these rules, and one draw needn't show every extreme that they name: Each row of matchings is a permutation of the 16 block numbers. block_device is a permutation of the 16 block numbers.
All inputs are finite; a program needn't handle non-finite values.
Results may differ from the reference program's by a relative error of at most 0.0027.
Values may be sent and summed in bfloat16 or wider, within the bound.
A program may use at most 64 MiB of HBM per device.

```python
import jax
import jax.numpy as jnp
from jax import lax

S = 512
LAGS = 128
TAPS = 129
M = 4
NB = 16
NT = 4096


def block_scale(stream_key, extent, cuts, smallest, largest):
    factor_of, own = 1.0, jax.random.fold_in(stream_key, 6)
    for axis_at, blocks in cuts:
        draws = jnp.exp(jax.random.uniform(jax.random.fold_in(own, axis_at), (blocks,), jnp.float32, smallest / len(cuts), largest / len(cuts)))
        factor_of = factor_of * jnp.repeat(draws, extent[axis_at] // blocks).reshape([-1 if axis == axis_at else 1 for axis in range(len(extent))])
    return factor_of


def gaussian(own_key, shape, width, most, split=(), kind=jnp.bfloat16):
    values = width * jax.random.normal(own_key, shape, jnp.float32)
    if split:
        values = values * block_scale(own_key, shape, split, -0.22, 0.18)
    return jnp.clip(values, -most, most).astype(kind)


def setup_inputs(seed: int = 0, part: int = 0) -> dict:
    key_list = jax.random.split(jax.random.key(seed), 5)
    part_keys = jax.random.split(jax.random.fold_in(key_list[4], part), 5)
    return {
        "noise_window": gaussian(part_keys[0], (S, NT), 1.0, 6.0, ((0, 16),), jnp.float32),
        "fir_taps": gaussian(part_keys[1], (S, TAPS), TAPS ** -0.5, 0.5, ((0, 16),), jnp.float32),
        "matchings": jax.vmap(lambda own: jax.random.permutation(own, NB))(jax.random.split(key_list[2], M)).reshape((M, NB)).astype(jnp.int32),
        "block_device": jax.random.permutation(key_list[3], NB).astype(jnp.int32),
    }


def whiten(signal, taps, lag_count):
    row_count, total = signal.shape
    tile_count = total // lag_count
    ntaps = taps.shape[1]
    tiles = signal.reshape(row_count, tile_count, lag_count)
    previous = jnp.concatenate([jnp.zeros((row_count, 1, lag_count), jnp.float32), tiles[:, :-1]], axis=1)
    joined = jnp.concatenate([previous, tiles], axis=2)
    inner = jnp.arange(2 * lag_count, dtype=jnp.int32)[:, None]
    outer = jnp.arange(lag_count, dtype=jnp.int32)[None, :]
    offset = lag_count + outer - inner
    valid = (offset >= 0) & (offset < ntaps)
    position = jnp.where(valid, offset, ntaps).astype(jnp.int32)
    padded = jnp.concatenate([taps, jnp.zeros((row_count, 1), jnp.float32)], axis=1)
    table = padded[:, position]
    result = jnp.einsum('rkj,rjo->rko', joined, table, precision=lax.Precision.HIGHEST)
    return result.reshape(row_count, total)

def invert(perm):
    count = perm.shape[-1]
    numbers = jnp.arange(count, dtype=jnp.int32)
    equal = perm[..., :, None] == numbers
    return lax.optimization_barrier(jnp.sum(jnp.where(equal, numbers[:, None], 0), axis=-2)).astype(jnp.int32)

def lookup(table, index):
    count = table.shape[-1]
    numbers = jnp.arange(count, dtype=jnp.int32)
    equal = index[..., :, None] == numbers
    return lax.optimization_barrier(jnp.sum(jnp.where(equal, table[..., None, :], 0), axis=-1)).astype(jnp.int32)

def partner_rows(matchings, block_device, row_count):
    match_count, block_count = matchings.shape
    block_size = row_count // block_count
    owner_of = invert(block_device)
    inverse_match = invert(matchings)
    held = jnp.broadcast_to(block_device, (match_count, block_count))
    partner_dev = lookup(owner_of, lookup(matchings, held))
    source_dev = lookup(owner_of, lookup(inverse_match, held))
    rowids = jnp.arange(row_count, dtype=jnp.int32)
    device_of = jnp.broadcast_to(rowids // block_size, (match_count, row_count))
    within = rowids % block_size
    prow = lookup(partner_dev, device_of) * block_size + within
    qrow = lookup(source_dev, device_of) * block_size + within
    return (prow.astype(jnp.int32), qrow.astype(jnp.int32))

def hankel_rows(window, lag_count):
    count = window.shape[0]
    repeated = jnp.broadcast_to(window[:, None, :], (count, lag_count + 1, 2 * lag_count))
    repeated = repeated.reshape(count, (lag_count + 1) * 2 * lag_count)
    repeated = repeated[:, :lag_count * (2 * lag_count + 1)]
    return repeated.reshape(count, lag_count, 2 * lag_count + 1)[:, :, :lag_count]

def reference(noise_window, fir_taps, matchings, block_device):
    row_count, total = noise_window.shape
    whitened = whiten(noise_window, fir_taps, LAGS)
    squashed = (whitened / (1.0 + jnp.abs(whitened))).astype(jnp.bfloat16)
    prow, qrow = partner_rows(matchings, block_device, row_count)
    extended = jnp.concatenate([squashed, jnp.zeros((row_count, LAGS), jnp.bfloat16)], axis=1)
    stacked = jnp.take(squashed, qrow.T, axis=0)
    match_count = matchings.shape[0]

    def tile_step(running, tile_index):
        start = (tile_index * LAGS).astype(jnp.int32)
        window = lax.dynamic_slice_in_dim(extended, start, 2 * LAGS, 1)
        part_a = lax.dynamic_slice_in_dim(stacked, start, LAGS, 2)
        hank = hankel_rows(window, LAGS)
        return (running + jnp.einsum('smj,sjl->sml', part_a.astype(jnp.float32), hank.astype(jnp.float32)), None)
    start_sum = jnp.zeros((row_count, match_count, LAGS), jnp.float32)
    result, _ = lax.scan(tile_step, start_sum, jnp.arange(total // LAGS, dtype=jnp.int32))
    flipped = jnp.transpose(result, (1, 0, 2))
    picked = jnp.take_along_axis(flipped, prow[:, :, None], axis=1)
    return picked / jnp.sqrt(jnp.float32(total))
```

```python
import functools

import jax
import jax.numpy as jnp
from jax import lax
from jax.experimental import pallas as pl
from jax.experimental.pallas import tpu as pltpu
from jax.sharding import PartitionSpec as P

LAGS = 128
F32 = jnp.float32
BF16 = jnp.bfloat16


def split_bf16(x):
    high = x.astype(BF16)
    low = (x - high.astype(F32)).astype(BF16)
    return high, low


def whiten_kernel(x_ref, taps_ref, sq_ref, rev_ref, prev_ref, xs_ref, ys_ref):
    rows, total = x_ref.shape
    tiles = total // LAGS
    pitch = tiles + 8
    zeros8 = jnp.zeros((8, LAGS), F32)
    for r in range(rows):
        xs_ref[pl.ds(r * pitch, 8), :] = zeros8
    for n in range(tiles):
        xs_ref[pl.ds(8 + n, rows, stride=pitch), :] = x_ref[:, n * LAGS:(n + 1) * LAGS]
    ys_ref[pl.ds(0, 8), :] = zeros8
    row_id = lax.broadcasted_iota(jnp.int32, (LAGS, LAGS), 0)
    col_id = lax.broadcasted_iota(jnp.int32, (LAGS, LAGS), 1)

    mirror = jnp.where(row_id + col_id == LAGS - 1, 1.0, 0.0).astype(BF16)

    def one_row(r, carry):
        base = pl.multiple_of(r * pitch, 8)
        cur = xs_ref[pl.ds(base + 8, tiles), :]
        before = xs_ref[pl.ds(base + 7, tiles), :]
        joined = jnp.concatenate([before, cur], axis=1)
        tap = taps_ref[pl.ds(r, 1), :]
        spread = jnp.broadcast_to(tap[:, :LAGS], (LAGS, LAGS))
        rolled = pltpu.roll(spread, 0, 1, stride=1, stride_axis=0)
        last = jnp.broadcast_to(tap[:, LAGS:LAGS + 1], (LAGS, LAGS))
        cur_t = jnp.where(col_id >= row_id, rolled, 0.0)
        prev_t = jnp.where(col_id < row_id, rolled, jnp.where(col_id == row_id, last, 0.0))
        table = jnp.concatenate([prev_t, cur_t], axis=0)
        xh, xl = split_bf16(joined)
        th, tl = split_bf16(table)
        dot = functools.partial(jnp.dot, preferred_element_type=F32)
        white = dot(xh, th) + (dot(xh, tl) + dot(xl, th))
        squashed = white / (1.0 + jnp.abs(white))
        ys_ref[pl.ds(8, tiles), :] = squashed
        shifted = ys_ref[pl.ds(7, tiles), :]
        out = pl.multiple_of(r * tiles, 16)
        rounded = squashed.astype(BF16)
        sq_ref[pl.ds(out, tiles), :] = rounded
        rev_ref[pl.ds(out, tiles), :] = dot(rounded, mirror).astype(BF16)
        prev_ref[pl.ds(out, tiles), :] = dot(shifted.astype(BF16), mirror).astype(BF16)
        return carry

    lax.fori_loop(0, rows, one_row, 0)


def whiten(noise, taps):
    rows, total = noise.shape
    tiles = total // LAGS
    shape = jax.ShapeDtypeStruct((rows * tiles, LAGS), BF16)
    return pl.pallas_call(
        whiten_kernel,
        out_shape=[shape] * 3,
        in_specs=[pl.BlockSpec(memory_space=pltpu.VMEM)] * 2,
        out_specs=[pl.BlockSpec(memory_space=pltpu.VMEM)] * 3,
        scratch_shapes=[
            pltpu.VMEM((rows * (tiles + 8), LAGS), F32),
            pltpu.VMEM((tiles + 8, LAGS), F32),
        ],
        compiler_params=pltpu.CompilerParams(vmem_limit_bytes=48 * 2**20),
    )(noise, taps)


def correlate_kernel(matchings_ref, device_ref, rev_ref, prev_ref, all_ref, out_ref, held, sems):
    matches, blocks = matchings_ref.shape
    rows = out_ref.shape[1]
    tiles = rev_ref.shape[0] // rows
    size = rows * tiles
    me = lax.axis_index("sta")
    mine = device_ref[me]
    copies = []
    for m in range(matches):
        wanted = matchings_ref[m, mine]
        partner = jnp.int32(0)
        for e in range(blocks):
            partner = jnp.where(device_ref[e] == wanted, e, partner)
        start = pl.multiple_of(partner * size, 16)
        copy = pltpu.make_async_copy(all_ref.at[pl.ds(start, size), :], held.at[m], sems.at[m])
        copy.start()
        copies.append(copy)
    for copy in copies:
        copy.wait()
    row_id = lax.broadcasted_iota(jnp.int32, (LAGS, LAGS), 0)
    col_id = lax.broadcasted_iota(jnp.int32, (LAGS, LAGS), 1)
    upper = col_id + row_id >= LAGS - 1
    scale = 1.0 / (tiles * LAGS) ** 0.5

    def one_row(r, carry):
        at = pl.multiple_of(r * tiles, 16)
        left = jnp.concatenate([rev_ref[pl.ds(at, tiles), :], prev_ref[pl.ds(at, tiles), :]], axis=1)
        for m in range(matches):
            right = held[m, pl.ds(at, tiles), :]
            gram = lax.dot_general(left, right, (((0,), (0,)), ((), ())), preferred_element_type=F32)
            chosen = jnp.where(upper, gram[:LAGS], gram[LAGS:])
            turned = pltpu.roll(chosen, 1, 1, stride=1, stride_axis=0)
            out_ref[m, pl.ds(r, 1), :] = jnp.sum(turned, axis=0, keepdims=True) * scale
        return carry

    lax.fori_loop(0, rows, one_row, 0)


def correlate(matchings, block_device, rev, prev, gathered, rows):
    matches = matchings.shape[0]
    return pl.pallas_call(
        correlate_kernel,
        out_shape=jax.ShapeDtypeStruct((matches, rows, LAGS), F32),
        in_specs=[pl.BlockSpec(memory_space=pltpu.SMEM)] * 2
        + [pl.BlockSpec(memory_space=pltpu.VMEM)] * 2
        + [pl.BlockSpec(memory_space=pl.ANY)],
        out_specs=pl.BlockSpec(memory_space=pltpu.VMEM),
        scratch_shapes=[
            pltpu.VMEM((matches,) + rev.shape, BF16),
            pltpu.SemaphoreType.DMA((matches,)),
        ],
        compiler_params=pltpu.CompilerParams(vmem_limit_bytes=48 * 2**20),
    )(matchings, block_device, rev, prev, gathered)


def per_device(noise_window, fir_taps, matchings, block_device):
    rows = noise_window.shape[0]
    sq, rev, prev = whiten(noise_window, fir_taps)
    gathered = lax.all_gather(sq, "sta", axis=0, tiled=True)
    return correlate(matchings, block_device, rev, prev, gathered, rows)


def solution(mesh):
    return jax.shard_map(
        per_device,
        mesh=mesh,
        in_specs=(P(("grp", "sta"), None), P(("grp", "sta"), None), P(), P()),
        out_specs=P(None, ("grp", "sta"), None),
        check_vma=False,
    )
```

```python
import functools

import jax
import jax.numpy as jnp
from jax import lax
from jax.experimental import pallas as pl
from jax.experimental.pallas import tpu as pltpu
from jax.sharding import PartitionSpec as P

LAGS = 128
F32 = jnp.float32
BF16 = jnp.bfloat16
SIB, ACROSS, DOWN, UP = range(4)


def split_bf16(x):
    high = x.astype(BF16)
    low = (x - high.astype(F32)).astype(BF16)
    return high, low


def kernel(width, part, noise_ref, taps_ref, matchings_ref, device_ref, out_ref,
           noise, taps, matchings, device, xs, ys, gathered, before, acc,
           in_sems, send_sems, recv_sems):
    blocks, parts, chunk, _ = gathered.shape
    rows, total = noise.shape
    matches = matchings.shape[0]
    tiles = total // LAGS
    pitch = tiles + 8
    me = lax.axis_index("sta")
    depth = blocks // (2 * width)
    core = me % 2
    y = (me // 2) % width
    z = me // (2 * width)
    sibling = me + 1 - 2 * core
    across = me + 2 - 4 * y
    down, up = me - 2 * width, me + 2 * width
    has_down, has_up = z > 0, z < depth - 1

    loads = [
        pltpu.make_async_copy(taps_ref, taps, in_sems.at[0]),
        pltpu.make_async_copy(matchings_ref, matchings, in_sems.at[1]),
        pltpu.make_async_copy(device_ref, device, in_sems.at[2]),
    ]

    def noise_load(k):
        span = pl.ds(pl.multiple_of(k * part, 8), part)
        return pltpu.make_async_copy(noise_ref.at[span, :], noise.at[span, :], in_sems.at[3 + k])

    noise_load(0).start()
    for load in loads:
        load.start()
    for k in range(1, parts):
        noise_load(k).start()

    barrier = pltpu.get_barrier_semaphore()
    greet = functools.partial(pl.semaphore_signal, barrier, inc=1)
    greet(device_id={"sta": sibling})
    if width > 1:
        greet(device_id={"sta": across})

    @pl.when(has_down)
    def _():
        greet(device_id={"sta": down})

    @pl.when(has_up)
    def _():
        greet(device_id={"sta": up})

    def copy(block, k, way, target):
        return pltpu.make_async_remote_copy(
            src_ref=gathered.at[block, k],
            dst_ref=gathered.at[block, k],
            send_sem=send_sems.at[way, block, k],
            recv_sem=recv_sems.at[block, k],
            device_id={"sta": target},
        )

    def landed(block, k):
        copy(block, k, SIB, sibling).wait_recv()

    row_id = lax.broadcasted_iota(jnp.int32, (LAGS, LAGS), 0)
    col_id = lax.broadcasted_iota(jnp.int32, (LAGS, LAGS), 1)
    upper = col_id >= row_id

    zeros8 = jnp.zeros((8, LAGS), F32)
    for r in range(part):
        xs[pl.ds(r * pitch, 8), :] = zeros8
        ys[pl.ds(r * pitch, 8), :] = zeros8
    for load in loads:
        load.wait()

    def whiten_part(k, carry):
        noise_load(k).wait()
        span = pl.ds(pl.multiple_of(k * part, 8), part)
        for n in range(tiles):
            xs[pl.ds(8 + n, part, stride=pitch), :] = noise[span, n * LAGS:(n + 1) * LAGS]
        tap_rows = taps[span, :]
        for r in range(part):
            cur = xs[pl.ds(r * pitch + 8, tiles), :]
            prior = xs[pl.ds(r * pitch + 7, tiles), :]
            joined = jnp.concatenate([prior, cur], axis=1)
            tap = tap_rows[r:r + 1]
            spread = jnp.broadcast_to(tap[:, :LAGS], (LAGS, LAGS))
            rolled = pltpu.roll(spread, 0, 1, stride=1, stride_axis=0)
            last = jnp.broadcast_to(tap[:, LAGS:LAGS + 1], (LAGS, LAGS))
            cur_t = jnp.where(upper, rolled, 0.0)
            prior_t = jnp.where(upper, jnp.where(col_id == row_id, last, 0.0), rolled)
            table = jnp.concatenate([prior_t, cur_t], axis=0)
            left = jnp.concatenate(split_bf16(joined), axis=0)
            right = jnp.concatenate(split_bf16(table), axis=1)
            four = jnp.dot(left, right, preferred_element_type=F32)
            white = four[:tiles, :LAGS] + (four[tiles:, :LAGS] + four[:tiles, LAGS:] + four[tiles:, LAGS:])
            squashed = white / (1.0 + jnp.abs(white))
            ys[pl.ds(r * pitch + 8, tiles), :] = squashed
            gathered[me, k, pl.ds(r * tiles, tiles), :] = squashed.astype(BF16)
            shifted = ys[pl.ds(r * pitch + 7, tiles), :]
            before[k, pl.ds(r * tiles, tiles), :] = shifted.astype(BF16)

        @pl.when(k == 0)
        def _():
            pl.semaphore_wait(barrier, 1 + (width > 1) + has_down.astype(jnp.int32) + has_up.astype(jnp.int32))

        if width > 1:
            copy(me, k, ACROSS, across).start()

        @pl.when(has_down)
        def _():
            copy(me, k, DOWN, down).start()

        @pl.when(has_up)
        def _():
            copy(me, k, UP, up).start()

        copy(me, k, SIB, sibling).start()
        return carry

    lax.fori_loop(0, parts, whiten_part, 0)

    def along(z_of, way, target, onward, k):
        block = z_of * 2 * width + y * 2 + core
        landed(block, k)
        if width > 1:
            copy(block, k, ACROSS, across).start()

        @pl.when(onward)
        def _():
            copy(block, k, way, target).start()

        copy(block, k, SIB, sibling).start()

    def from_across(z_of, k):
        block = z_of * 2 * width + (1 - y) * 2 + core
        landed(block, k)
        copy(block, k, SIB, sibling).start()

    def round_part(i, carry):
        d = i // parts
        k = i % parts

        @pl.when((d > 0) & (z - d >= 0))
        def _():
            along(z - d, UP, up, has_up, k)

        @pl.when((d > 0) & (z + d < depth))
        def _():
            along(z + d, DOWN, down, has_down, k)

        if width > 1:
            @pl.when((d > 0) & (z - d + 1 >= 0))
            def _():
                from_across(z - d + 1, k)

            @pl.when((d > 1) & (z + d - 1 < depth))
            def _():
                from_across(z + d - 1, k)

        return carry

    lax.fori_loop(parts, (depth + 1) * parts, round_part, 0)

    def last_part(i, carry):
        pair = i // parts
        k = i % parts
        landed(2 * pair + 1 - core, k)
        return carry

    lax.fori_loop(0, blocks // 2 * parts, last_part, 0)

    partners = []
    mine = device[me]
    for m in range(matches):
        wanted = matchings[m, mine]
        partner = jnp.int32(0)
        for e in range(blocks):
            partner = jnp.where(device[e] == wanted, e, partner)
        partners.append(partner)

    def correlate_row(r, carry):
        k = r // part
        span = pl.ds(pl.multiple_of((r % part) * tiles, 16), tiles)
        left = jnp.concatenate([gathered[me, k, span, :], before[k, span, :]], axis=1)
        right = jnp.concatenate([gathered[partner, k, span, :] for partner in partners], axis=1)
        gram = lax.dot_general(left, right, (((0,), (0,)), ((), ())), preferred_element_type=F32)
        for m in range(matches):
            lanes = slice(m * LAGS, (m + 1) * LAGS)
            chosen = jnp.where(upper, gram[:LAGS, lanes], gram[LAGS:, lanes])
            terms = [chosen[:8]]
            for g in range(8, LAGS, 8):
                terms.append(pltpu.roll(chosen[g:g + 8], LAGS - g, 1))
            while len(terms) > 1:
                terms = [a + b for a, b in zip(terms[::2], terms[1::2])]
            acc[pl.ds(pl.multiple_of((m * rows + r) * 8, 8), 8), :] = terms[0]
        return carry

    lax.fori_loop(0, rows, correlate_row, 0, unroll=2)

    scale = 1.0 / total ** 0.5
    for m in range(matches):
        lags = acc[pl.ds(m * rows * 8, rows, stride=8), :]
        for s in range(1, 8):
            lags += pltpu.roll(acc[pl.ds(m * rows * 8 + s, rows, stride=8), :], LAGS - s, 1)
        out_ref[m] = lags * scale

    def sent(i, carry):
        block = i // parts
        k = i % parts
        b_core = block % 2
        b_y = (block // 2) % width
        b_z = block // (2 * width)
        straight = (b_core == core) & (b_y == y)

        @pl.when(b_core == core)
        def _():
            copy(block, k, SIB, sibling).wait_send()

        if width > 1:
            @pl.when(straight)
            def _():
                copy(block, k, ACROSS, across).wait_send()

        @pl.when(straight & has_up & (b_z <= z))
        def _():
            copy(block, k, UP, up).wait_send()

        @pl.when(straight & has_down & (b_z >= z))
        def _():
            copy(block, k, DOWN, down).wait_send()

        return carry

    lax.fori_loop(0, blocks * parts, sent, 0)


def per_device(width, noise_window, fir_taps, matchings, block_device):
    rows, total = noise_window.shape
    matches, blocks = matchings.shape
    tiles = total // LAGS
    part = 8 if rows % 8 == 0 else rows
    parts = rows // part
    return pl.pallas_call(
        functools.partial(kernel, width, part),
        out_shape=jax.ShapeDtypeStruct((matches, rows, LAGS), F32),
        in_specs=[pl.BlockSpec(memory_space=pl.ANY)] * 4,
        out_specs=pl.BlockSpec(memory_space=pltpu.VMEM),
        scratch_shapes=[
            pltpu.VMEM((rows, total), F32),
            pltpu.VMEM(fir_taps.shape, F32),
            pltpu.SMEM(matchings.shape, jnp.int32),
            pltpu.SMEM(block_device.shape, jnp.int32),
            pltpu.VMEM((part * (tiles + 8), LAGS), F32),
            pltpu.VMEM((part * (tiles + 8), LAGS), F32),
            pltpu.VMEM((blocks, parts, part * tiles, LAGS), BF16),
            pltpu.VMEM((parts, part * tiles, LAGS), BF16),
            pltpu.VMEM((matches * rows * 8, LAGS), F32),
            pltpu.SemaphoreType.DMA((3 + parts,)),
            pltpu.SemaphoreType.DMA((4, blocks, parts)),
            pltpu.SemaphoreType.DMA((blocks, parts)),
        ],
        compiler_params=pltpu.CompilerParams(
            collective_id=0, has_side_effects=True, vmem_limit_bytes=48 * 2**20
        ),
    )(noise_window, fir_taps, matchings, block_device)


def plane_width(mesh):
    line = mesh.devices.reshape(mesh.shape["grp"], -1)[0]
    places = [getattr(d, "coords", None) for d in line]
    if any(p is None for p in places):
        return 1
    width = len({tuple(p[:2]) for p in places})
    return width if width == 2 and len(places) % 4 == 0 else 1


def solution(mesh):
    return jax.shard_map(
        functools.partial(per_device, plane_width(mesh)),
        mesh=mesh,
        in_specs=(P(("grp", "sta"), None), P(("grp", "sta"), None), P(), P()),
        out_specs=P(None, ("grp", "sta"), None),
        check_vma=False,
    )
```

```python
import functools

import jax
import jax.numpy as jnp
from jax import lax
from jax.experimental import pallas as pl
from jax.experimental.pallas import tpu as pltpu
from jax.sharding import PartitionSpec as P

LAGS = 128
F32 = jnp.float32
BF16 = jnp.bfloat16
SIB, ACROSS, DOWN, UP = range(4)
UNROLL = 4


def split_bf16(x):
    high = x.astype(BF16)
    low = (x - high.astype(F32)).astype(BF16)
    return high, low


def kernel(width, part, noise_ref, taps_ref, matchings_ref, device_ref, out_ref,
           noise, taps, matchings, device, xs, ys, own, before, acc,
           in_sems, send_sems, recv_sems, *gathered):
    parts = len(gathered)
    blocks = gathered[0].shape[0]
    rows, total = noise.shape
    matches = matchings.shape[0]
    tiles = total // LAGS
    pitch = tiles + 8
    me = lax.axis_index("sta")
    depth = blocks // (2 * width)
    core = me % 2
    y = (me // 2) % width
    z = me // (2 * width)
    sibling = me + 1 - 2 * core
    across = me + 2 - 4 * y
    down, up = me - 2 * width, me + 2 * width
    has_down, has_up = z > 0, z < depth - 1

    loads = [
        pltpu.make_async_copy(taps_ref, taps, in_sems.at[0]),
        pltpu.make_async_copy(matchings_ref, matchings, in_sems.at[1]),
        pltpu.make_async_copy(device_ref, device, in_sems.at[2]),
    ]

    def noise_load(k):
        span = pl.ds(pl.multiple_of(k * part, 8), part)
        return pltpu.make_async_copy(noise_ref.at[span, :], noise.at[span, :], in_sems.at[3 + k])

    noise_load(0).start()
    for load in loads:
        load.start()
    for k in range(1, parts):
        noise_load(k).start()

    barrier = pltpu.get_barrier_semaphore()
    greet = functools.partial(pl.semaphore_signal, barrier, inc=1)
    greet(device_id={"sta": sibling})
    if width > 1:
        greet(device_id={"sta": across})

    @pl.when(has_down)
    def _():
        greet(device_id={"sta": down})

    @pl.when(has_up)
    def _():
        greet(device_id={"sta": up})

    def copy(block, k, way, target):
        return pltpu.make_async_remote_copy(
            src_ref=gathered[k].at[block],
            dst_ref=gathered[k].at[block],
            send_sem=send_sems.at[way, block, k],
            recv_sem=recv_sems.at[block, k],
            device_id={"sta": target},
        )

    def landed(block, k):
        copy(block, k, SIB, sibling).wait_recv()

    row_id = lax.broadcasted_iota(jnp.int32, (LAGS, LAGS), 0)
    col_id = lax.broadcasted_iota(jnp.int32, (LAGS, LAGS), 1)
    upper = col_id >= row_id

    zeros8 = jnp.zeros((8, LAGS), F32)
    for r in range(part):
        xs[pl.ds(r * pitch, 8), :] = zeros8
        ys[pl.ds(r * pitch, 8), :] = zeros8
    for load in loads:
        load.wait()

    def whiten_part(k, carry):
        noise_load(k).wait()
        span = pl.ds(pl.multiple_of(k * part, 8), part)
        for n in range(tiles):
            xs[pl.ds(8 + n, part, stride=pitch), :] = noise[span, n * LAGS:(n + 1) * LAGS]
        tap_rows = taps[span, :]
        for r in range(part):
            cur = xs[pl.ds(r * pitch + 8, tiles), :]
            prior = xs[pl.ds(r * pitch + 7, tiles), :]
            joined = jnp.concatenate([prior, cur], axis=1)
            tap = tap_rows[r:r + 1]
            spread = jnp.broadcast_to(tap[:, :LAGS], (LAGS, LAGS))
            rolled = pltpu.roll(spread, 0, 1, stride=1, stride_axis=0)
            last = jnp.broadcast_to(tap[:, LAGS:LAGS + 1], (LAGS, LAGS))
            cur_t = jnp.where(upper, rolled, 0.0)
            prior_t = jnp.where(upper, jnp.where(col_id == row_id, last, 0.0), rolled)
            table = jnp.concatenate([prior_t, cur_t], axis=0)
            left = jnp.concatenate(split_bf16(joined), axis=0)
            right = jnp.concatenate(split_bf16(table), axis=1)
            four = jnp.dot(left, right, preferred_element_type=F32)
            white = four[:tiles, :LAGS] + (four[tiles:, :LAGS] + four[:tiles, LAGS:] + four[tiles:, LAGS:])
            squashed = white / (1.0 + jnp.abs(white))
            ys[pl.ds(r * pitch + 8, tiles), :] = squashed
            own[k, pl.ds(r * tiles, tiles), :] = squashed.astype(BF16)
            shifted = ys[pl.ds(r * pitch + 7, tiles), :]
            before[k, pl.ds(r * tiles, tiles), :] = shifted.astype(BF16)

        @pl.when(k == 0)
        def _():
            pl.semaphore_wait(barrier, 1 + (width > 1) + has_down.astype(jnp.int32) + has_up.astype(jnp.int32))

        for at in range(parts):
            @pl.when(k == at)
            def _():
                gathered[at][me] = own[at]
                if width > 1:
                    copy(me, at, ACROSS, across).start()

                @pl.when(has_down)
                def _():
                    copy(me, at, DOWN, down).start()

                @pl.when(has_up)
                def _():
                    copy(me, at, UP, up).start()

                copy(me, at, SIB, sibling).start()

        return carry

    lax.fori_loop(0, parts, whiten_part, 0)

    paired = width > 1 and depth % 2 == 0
    mate = z + 1 - 2 * (z % 2)

    def late(k):
        return paired and 2 * k >= parts and parts > 1

    def along(z_of, way, target, onward, k):
        block = z_of * 2 * width + y * 2 + core
        landed(block, k)

        @pl.when(onward)
        def _():
            copy(block, k, way, target).start()

        if width > 1:
            @pl.when(jnp.logical_not(late(k) & (z_of == mate)))
            def _():
                copy(block, k, ACROSS, across).start()

        copy(block, k, SIB, sibling).start()

    def from_across(z_of, k):
        block = z_of * 2 * width + (1 - y) * 2 + core
        landed(block, k)
        if late(k):
            @pl.when((z_of == z) & (mate > z))
            def _():
                copy(block, k, UP, up).start()

            @pl.when((z_of == z) & (mate < z))
            def _():
                copy(block, k, DOWN, down).start()

        copy(block, k, SIB, sibling).start()

    def round_part(d, k):
        @pl.when(z - d >= 0)
        def _():
            along(z - d, UP, up, has_up, k)

        @pl.when(z + d < depth)
        def _():
            along(z + d, DOWN, down, has_down, k)

        if width > 1:
            @pl.when(z - d + 1 >= 0)
            def _():
                from_across(z - d + 1, k)

            @pl.when((d > 1) & (z + d - 1 < depth))
            def _():
                from_across(z + d - 1, k)

    def one_round(d, carry):
        for k in range(parts):
            round_part(d, k)
        return carry

    lax.fori_loop(1, depth, one_round, 0)

    partners = []
    mine = device[me]
    for m in range(matches):
        wanted = matchings[m, mine]
        partner = jnp.int32(0)
        for e in range(blocks):
            partner = jnp.where(device[e] == wanted, e, partner)
        partners.append(partner)

    def correlate_row(k, r, carry):
        span = pl.ds(pl.multiple_of(r * tiles, 16), tiles)
        left = jnp.concatenate([own[k, span, :], before[k, span, :]], axis=1)
        right = jnp.concatenate([gathered[k][partner, span, :] for partner in partners], axis=1)
        gram = lax.dot_general(left, right, (((0,), (0,)), ((), ())), preferred_element_type=F32)
        for m in range(matches):
            lanes = slice(m * LAGS, (m + 1) * LAGS)
            chosen = jnp.where(upper, gram[:LAGS, lanes], gram[LAGS:, lanes])
            terms = [chosen[:8]]
            for g in range(8, LAGS, 8):
                terms.append(pltpu.roll(chosen[g:g + 8], LAGS - g, 1))
            while len(terms) > 1:
                terms = [a + b for a, b in zip(terms[::2], terms[1::2])]
            acc[pl.ds(pl.multiple_of((m * rows + k * part + r) * 8, 8), 8), :] = terms[0]
        return carry

    def finish(k):
        def one(pair, carry):
            landed(2 * pair + 1 - core, k)
            return carry

        lax.fori_loop(0, blocks // 2, one, 0)
        lax.fori_loop(0, part, functools.partial(correlate_row, k), 0, unroll=UNROLL)

    for k in range(parts):
        round_part(jnp.int32(depth), k)
        if k > 0:
            finish(k - 1)
    finish(parts - 1)

    scale = 1.0 / total ** 0.5
    for m in range(matches):
        lags = acc[pl.ds(m * rows * 8, rows, stride=8), :]
        for s in range(1, 8):
            lags += pltpu.roll(acc[pl.ds(m * rows * 8 + s, rows, stride=8), :], LAGS - s, 1)
        out_ref[m] = lags * scale

    def sent(block, carry):
        b_core = block % 2
        b_y = (block // 2) % width
        b_z = block // (2 * width)
        straight = (b_core == core) & (b_y == y)
        for k in range(parts):
            @pl.when(b_core == core)
            def _():
                copy(block, k, SIB, sibling).wait_send()

            turned = jnp.bool_(False)
            if late(k):
                turned = (b_core == core) & (b_y != y) & (b_z == z)
            if width > 1:
                @pl.when(straight & jnp.logical_not(late(k) & (b_z == mate)))
                def _():
                    copy(block, k, ACROSS, across).wait_send()

            @pl.when((straight & has_up & (b_z <= z)) | (turned & (mate > z)))
            def _():
                copy(block, k, UP, up).wait_send()

            @pl.when((straight & has_down & (b_z >= z)) | (turned & (mate < z)))
            def _():
                copy(block, k, DOWN, down).wait_send()

        return carry

    lax.fori_loop(0, blocks, sent, 0)


def per_device(width, noise_window, fir_taps, matchings, block_device):
    rows, total = noise_window.shape
    matches, blocks = matchings.shape
    tiles = total // LAGS
    part = 8 if rows % 8 == 0 else rows
    parts = rows // part
    return pl.pallas_call(
        functools.partial(kernel, width, part),
        out_shape=jax.ShapeDtypeStruct((matches, rows, LAGS), F32),
        in_specs=[pl.BlockSpec(memory_space=pltpu.HBM)] * 4,
        out_specs=pl.BlockSpec(memory_space=pltpu.VMEM),
        scratch_shapes=[
            pltpu.VMEM((rows, total), F32),
            pltpu.VMEM(fir_taps.shape, F32),
            pltpu.SMEM(matchings.shape, jnp.int32),
            pltpu.SMEM(block_device.shape, jnp.int32),
            pltpu.VMEM((part * (tiles + 8), LAGS), F32),
            pltpu.VMEM((part * (tiles + 8), LAGS), F32),
            pltpu.VMEM((parts, part * tiles, LAGS), BF16),
            pltpu.VMEM((parts, part * tiles, LAGS), BF16),
            pltpu.VMEM((matches * rows * 8, LAGS), F32),
            pltpu.SemaphoreType.DMA((3 + parts,)),
            pltpu.SemaphoreType.DMA((4, blocks, parts)),
            pltpu.SemaphoreType.DMA((blocks, parts)),
        ] + [pltpu.VMEM((blocks, part * tiles, LAGS), BF16)] * parts,
        compiler_params=pltpu.CompilerParams(
            collective_id=0, has_side_effects=True, vmem_limit_bytes=48 * 2**20
        ),
    )(noise_window, fir_taps, matchings, block_device)


def plane_width(mesh):
    line = mesh.devices.reshape(mesh.shape["grp"], -1)[0]
    places = [getattr(d, "coords", None) for d in line]
    if any(p is None for p in places):
        return 1
    width = len({tuple(p[:2]) for p in places})
    return width if width == 2 and len(places) % 4 == 0 else 1


def solution(mesh):
    return jax.shard_map(
        functools.partial(per_device, plane_width(mesh)),
        mesh=mesh,
        in_specs=(P(("grp", "sta"), None), P(("grp", "sta"), None), P(), P()),
        out_specs=P(None, ("grp", "sta"), None),
        check_vma=False,
    )
```

```python
import functools

import jax
import jax.numpy as jnp
from jax import lax
from jax.experimental import pallas as pl
from jax.experimental.pallas import tpu as pltpu
from jax.sharding import PartitionSpec as P

LAGS = 128
F32 = jnp.float32
BF16 = jnp.bfloat16
SIB, ACROSS, DOWN, UP = range(4)
UNROLL = 4


def split_bf16(x):
    high = x.astype(BF16)
    low = (x - high.astype(F32)).astype(BF16)
    return high, low


def kernel(width, part, noise_ref, taps_ref, matchings_ref, device_ref, out_ref,
           noise, taps, matchings, device, xs, ys, own, before, acc,
           in_sems, send_sems, recv_sems, *gathered):
    parts = len(gathered)
    blocks = gathered[0].shape[0]
    rows, total = noise.shape
    matches = matchings.shape[0]
    tiles = total // LAGS
    pitch = tiles + 8
    me = lax.axis_index("sta")
    depth = blocks // (2 * width)
    core = me % 2
    y = (me // 2) % width
    z = me // (2 * width)
    sibling = me + 1 - 2 * core
    across = me + 2 - 4 * y
    down, up = me - 2 * width, me + 2 * width
    has_down, has_up = z > 0, z < depth - 1

    loads = [
        pltpu.make_async_copy(taps_ref, taps, in_sems.at[0]),
        pltpu.make_async_copy(matchings_ref, matchings, in_sems.at[1]),
        pltpu.make_async_copy(device_ref, device, in_sems.at[2]),
    ]

    def noise_load(k):
        span = pl.ds(pl.multiple_of(k * part, 8), part)
        return pltpu.make_async_copy(noise_ref.at[span, :], noise.at[span, :], in_sems.at[3 + k])

    noise_load(0).start()
    for load in loads:
        load.start()
    for k in range(1, parts):
        noise_load(k).start()

    barrier = pltpu.get_barrier_semaphore()
    greet = functools.partial(pl.semaphore_signal, barrier, inc=1)
    greet(device_id={"sta": sibling})
    if width > 1:
        greet(device_id={"sta": across})

    @pl.when(has_down)
    def _():
        greet(device_id={"sta": down})

    @pl.when(has_up)
    def _():
        greet(device_id={"sta": up})

    def copy(block, k, way, target):
        return pltpu.make_async_remote_copy(
            src_ref=gathered[k].at[block],
            dst_ref=gathered[k].at[block],
            send_sem=send_sems.at[way, block, k],
            recv_sem=recv_sems.at[block, k],
            device_id={"sta": target},
        )

    def landed(block, k):
        copy(block, k, SIB, sibling).wait_recv()

    row_id = lax.broadcasted_iota(jnp.int32, (LAGS, LAGS), 0)
    col_id = lax.broadcasted_iota(jnp.int32, (LAGS, LAGS), 1)
    upper = col_id >= row_id

    zeros8 = jnp.zeros((8, LAGS), F32)
    for r in range(part):
        xs[pl.ds(r * pitch, 8), :] = zeros8
        ys[pl.ds(r * pitch, 8), :] = zeros8
    for load in loads:
        load.wait()

    def whiten_part(k, carry):
        noise_load(k).wait()
        span = pl.ds(pl.multiple_of(k * part, 8), part)
        for n in range(tiles):
            xs[pl.ds(8 + n, part, stride=pitch), :] = noise[span, n * LAGS:(n + 1) * LAGS]
        tap_rows = taps[span, :]
        for r in range(part):
            cur = xs[pl.ds(r * pitch + 8, tiles), :]
            prior = xs[pl.ds(r * pitch + 7, tiles), :]
            joined = jnp.concatenate([prior, cur], axis=1)
            tap = tap_rows[r:r + 1]
            spread = jnp.broadcast_to(tap[:, :LAGS], (LAGS, LAGS))
            rolled = pltpu.roll(spread, 0, 1, stride=1, stride_axis=0)
            last = jnp.broadcast_to(tap[:, LAGS:LAGS + 1], (LAGS, LAGS))
            cur_t = jnp.where(upper, rolled, 0.0)
            prior_t = jnp.where(upper, jnp.where(col_id == row_id, last, 0.0), rolled)
            table = jnp.concatenate([prior_t, cur_t], axis=0)
            left = jnp.concatenate(split_bf16(joined), axis=0)
            right = jnp.concatenate(split_bf16(table), axis=1)
            four = jnp.dot(left, right, preferred_element_type=F32)
            white = four[:tiles, :LAGS] + (four[tiles:, :LAGS] + four[:tiles, LAGS:] + four[tiles:, LAGS:])
            squashed = white / (1.0 + jnp.abs(white))
            ys[pl.ds(r * pitch + 8, tiles), :] = squashed
            own[k, pl.ds(r * tiles, tiles), :] = squashed.astype(BF16)
            shifted = ys[pl.ds(r * pitch + 7, tiles), :]
            before[k, pl.ds(r * tiles, tiles), :] = shifted.astype(BF16)

        @pl.when(k == 0)
        def _():
            pl.semaphore_wait(barrier, 1 + (width > 1) + has_down.astype(jnp.int32) + has_up.astype(jnp.int32))

        for at in range(parts):
            @pl.when(k == at)
            def _():
                gathered[at][me] = own[at]
                if width > 1:
                    copy(me, at, ACROSS, across).start()

                @pl.when(has_down)
                def _():
                    copy(me, at, DOWN, down).start()

                @pl.when(has_up)
                def _():
                    copy(me, at, UP, up).start()

                copy(me, at, SIB, sibling).start()
                if at >= 2 and depth > 1:
                    round_part(jnp.int32(1), at - 2)

        return carry

    paired = width > 1 and depth % 2 == 0
    mate = z + 1 - 2 * (z % 2)

    def late(k):
        return paired and 2 * k >= parts and parts > 1

    def along(z_of, way, target, onward, k):
        block = z_of * 2 * width + y * 2 + core
        landed(block, k)

        @pl.when(onward)
        def _():
            copy(block, k, way, target).start()

        if width > 1:
            @pl.when(jnp.logical_not(late(k) & (z_of == mate)))
            def _():
                copy(block, k, ACROSS, across).start()

        copy(block, k, SIB, sibling).start()

    def from_across(z_of, k):
        block = z_of * 2 * width + (1 - y) * 2 + core
        landed(block, k)
        if late(k):
            @pl.when((z_of == z) & (mate > z))
            def _():
                copy(block, k, UP, up).start()

            @pl.when((z_of == z) & (mate < z))
            def _():
                copy(block, k, DOWN, down).start()

        copy(block, k, SIB, sibling).start()

    def round_part(d, k):
        @pl.when(z - d >= 0)
        def _():
            along(z - d, UP, up, has_up, k)

        @pl.when(z + d < depth)
        def _():
            along(z + d, DOWN, down, has_down, k)

        if width > 1:
            @pl.when(z - d + 1 >= 0)
            def _():
                from_across(z - d + 1, k)

            @pl.when((d > 1) & (z + d - 1 < depth))
            def _():
                from_across(z + d - 1, k)

    def one_round(d, carry):
        for k in range(parts):
            round_part(d, k)
        return carry

    lax.fori_loop(0, parts, whiten_part, 0)

    if depth > 1:
        for k in range(max(parts - 2, 0), parts):
            round_part(jnp.int32(1), k)
        lax.fori_loop(2, depth, one_round, 0)

    partners = []
    mine = device[me]
    for m in range(matches):
        wanted = matchings[m, mine]
        partner = jnp.int32(0)
        for e in range(blocks):
            partner = jnp.where(device[e] == wanted, e, partner)
        partners.append(partner)

    def correlate_row(k, r, carry):
        span = pl.ds(pl.multiple_of(r * tiles, 16), tiles)
        left = jnp.concatenate([own[k, span, :], before[k, span, :]], axis=1)
        right = jnp.concatenate([gathered[k][partner, span, :] for partner in partners], axis=1)
        gram = lax.dot_general(left, right, (((0,), (0,)), ((), ())), preferred_element_type=F32)
        for m in range(matches):
            lanes = slice(m * LAGS, (m + 1) * LAGS)
            chosen = jnp.where(upper, gram[:LAGS, lanes], gram[LAGS:, lanes])
            terms = [chosen[:8]]
            for g in range(8, LAGS, 8):
                terms.append(pltpu.roll(chosen[g:g + 8], LAGS - g, 1))
            while len(terms) > 1:
                terms = [a + b for a, b in zip(terms[::2], terms[1::2])]
            acc[pl.ds(pl.multiple_of((m * rows + k * part + r) * 8, 8), 8), :] = terms[0]
        return carry

    def finish(k):
        def one(pair, carry):
            landed(2 * pair + 1 - core, k)
            return carry

        lax.fori_loop(0, blocks // 2, one, 0)
        lax.fori_loop(0, part, functools.partial(correlate_row, k), 0, unroll=UNROLL)

    for k in range(parts):
        round_part(jnp.int32(depth), k)
        if k > 0:
            finish(k - 1)
    finish(parts - 1)

    scale = 1.0 / total ** 0.5
    for m in range(matches):
        lags = acc[pl.ds(m * rows * 8, rows, stride=8), :]
        for s in range(1, 8):
            lags += pltpu.roll(acc[pl.ds(m * rows * 8 + s, rows, stride=8), :], LAGS - s, 1)
        out_ref[m] = lags * scale

    def sent(block, carry):
        b_core = block % 2
        b_y = (block // 2) % width
        b_z = block // (2 * width)
        straight = (b_core == core) & (b_y == y)
        for k in range(parts):
            @pl.when(b_core == core)
            def _():
                copy(block, k, SIB, sibling).wait_send()

            turned = jnp.bool_(False)
            if late(k):
                turned = (b_core == core) & (b_y != y) & (b_z == z)
            if width > 1:
                @pl.when(straight & jnp.logical_not(late(k) & (b_z == mate)))
                def _():
                    copy(block, k, ACROSS, across).wait_send()

            @pl.when((straight & has_up & (b_z <= z)) | (turned & (mate > z)))
            def _():
                copy(block, k, UP, up).wait_send()

            @pl.when((straight & has_down & (b_z >= z)) | (turned & (mate < z)))
            def _():
                copy(block, k, DOWN, down).wait_send()

        return carry

    lax.fori_loop(0, blocks, sent, 0)


def per_device(width, noise_window, fir_taps, matchings, block_device):
    rows, total = noise_window.shape
    matches, blocks = matchings.shape
    tiles = total // LAGS
    part = 8 if rows % 8 == 0 else rows
    parts = rows // part
    return pl.pallas_call(
        functools.partial(kernel, width, part),
        out_shape=jax.ShapeDtypeStruct((matches, rows, LAGS), F32),
        in_specs=[pl.BlockSpec(memory_space=pltpu.HBM)] * 4,
        out_specs=pl.BlockSpec(memory_space=pltpu.VMEM),
        scratch_shapes=[
            pltpu.VMEM((rows, total), F32),
            pltpu.VMEM(fir_taps.shape, F32),
            pltpu.SMEM(matchings.shape, jnp.int32),
            pltpu.SMEM(block_device.shape, jnp.int32),
            pltpu.VMEM((part * (tiles + 8), LAGS), F32),
            pltpu.VMEM((part * (tiles + 8), LAGS), F32),
            pltpu.VMEM((parts, part * tiles, LAGS), BF16),
            pltpu.VMEM((parts, part * tiles, LAGS), BF16),
            pltpu.VMEM((matches * rows * 8, LAGS), F32),
            pltpu.SemaphoreType.DMA((3 + parts,)),
            pltpu.SemaphoreType.DMA((4, blocks, parts)),
            pltpu.SemaphoreType.DMA((blocks, parts)),
        ] + [pltpu.VMEM((blocks, part * tiles, LAGS), BF16)] * parts,
        compiler_params=pltpu.CompilerParams(
            collective_id=0, has_side_effects=True, vmem_limit_bytes=48 * 2**20
        ),
    )(noise_window, fir_taps, matchings, block_device)


def plane_width(mesh):
    line = mesh.devices.reshape(mesh.shape["grp"], -1)[0]
    places = [getattr(d, "coords", None) for d in line]
    if any(p is None for p in places):
        return 1
    width = len({tuple(p[:2]) for p in places})
    return width if width == 2 and len(places) % 4 == 0 else 1


def solution(mesh):
    return jax.shard_map(
        functools.partial(per_device, plane_width(mesh)),
        mesh=mesh,
        in_specs=(P(("grp", "sta"), None), P(("grp", "sta"), None), P(), P()),
        out_specs=P(None, ("grp", "sta"), None),
        check_vma=False,
    )
```

```python
import functools

import jax
import jax.numpy as jnp
from jax import lax
from jax.experimental import pallas as pl
from jax.experimental.pallas import tpu as pltpu
from jax.sharding import PartitionSpec as P

LAGS = 128
F32 = jnp.float32
BF16 = jnp.bfloat16
SIB, ACROSS, DOWN, UP = range(4)
UNROLL = 8


def split_bf16(x):
    high = x.astype(BF16)
    low = (x - high.astype(F32)).astype(BF16)
    return high, low


def kernel(width, part, noise_ref, taps_ref, matchings_ref, device_ref, out_ref,
           noise, taps, matchings, device, xs, ys, own, before, acc,
           in_sems, send_sems, recv_sems, *gathered):
    parts = len(gathered)
    blocks = gathered[0].shape[0]
    rows, total = noise.shape
    matches = matchings.shape[0]
    tiles = total // LAGS
    pitch = tiles + 8
    me = lax.axis_index("sta")
    depth = blocks // (2 * width)
    core = me % 2
    y = (me // 2) % width
    z = me // (2 * width)
    sibling = me + 1 - 2 * core
    across = me + 2 - 4 * y
    down, up = me - 2 * width, me + 2 * width
    has_down, has_up = z > 0, z < depth - 1

    loads = [
        pltpu.make_async_copy(taps_ref, taps, in_sems.at[0]),
        pltpu.make_async_copy(matchings_ref, matchings, in_sems.at[1]),
        pltpu.make_async_copy(device_ref, device, in_sems.at[2]),
    ]

    def noise_load(k):
        span = pl.ds(pl.multiple_of(k * part, 8), part)
        return pltpu.make_async_copy(noise_ref.at[span, :], noise.at[span, :], in_sems.at[3 + k])

    noise_load(0).start()
    for load in loads:
        load.start()
    for k in range(1, parts):
        noise_load(k).start()

    barrier = pltpu.get_barrier_semaphore()
    greet = functools.partial(pl.semaphore_signal, barrier, inc=1)
    greet(device_id={"sta": sibling})
    if width > 1:
        greet(device_id={"sta": across})

    @pl.when(has_down)
    def _():
        greet(device_id={"sta": down})

    @pl.when(has_up)
    def _():
        greet(device_id={"sta": up})

    def copy(block, k, way, target):
        return pltpu.make_async_remote_copy(
            src_ref=gathered[k].at[block],
            dst_ref=gathered[k].at[block],
            send_sem=send_sems.at[way, block, k],
            recv_sem=recv_sems.at[block, k],
            device_id={"sta": target},
        )

    def landed(block, k):
        copy(block, k, SIB, sibling).wait_recv()

    row_id = lax.broadcasted_iota(jnp.int32, (LAGS, LAGS), 0)
    col_id = lax.broadcasted_iota(jnp.int32, (LAGS, LAGS), 1)
    upper = col_id >= row_id

    zeros8 = jnp.zeros((8, LAGS), F32)
    for r in range(part):
        xs[pl.ds(r * pitch, 8), :] = zeros8
        ys[pl.ds(r * pitch, 8), :] = zeros8
    for load in loads:
        load.wait()

    def whiten_part(k, carry):
        noise_load(k).wait()
        span = pl.ds(pl.multiple_of(k * part, 8), part)
        for n in range(tiles):
            xs[pl.ds(8 + n, part, stride=pitch), :] = noise[span, n * LAGS:(n + 1) * LAGS]
        tap_rows = taps[span, :]
        for r in range(part):
            cur = xs[pl.ds(r * pitch + 8, tiles), :]
            prior = xs[pl.ds(r * pitch + 7, tiles), :]
            joined = jnp.concatenate([prior, cur], axis=1)
            tap = tap_rows[r:r + 1]
            spread = jnp.broadcast_to(tap[:, :LAGS], (LAGS, LAGS))
            rolled = pltpu.roll(spread, 0, 1, stride=1, stride_axis=0)
            last = jnp.broadcast_to(tap[:, LAGS:LAGS + 1], (LAGS, LAGS))
            cur_t = jnp.where(upper, rolled, 0.0)
            prior_t = jnp.where(upper, jnp.where(col_id == row_id, last, 0.0), rolled)
            table = jnp.concatenate([prior_t, cur_t], axis=0)
            left = jnp.concatenate(split_bf16(joined), axis=0)
            right = jnp.concatenate(split_bf16(table), axis=1)
            four = jnp.dot(left, right, preferred_element_type=F32)
            white = four[:tiles, :LAGS] + (four[tiles:, :LAGS] + four[:tiles, LAGS:] + four[tiles:, LAGS:])
            squashed = white / (1.0 + jnp.abs(white))
            ys[pl.ds(r * pitch + 8, tiles), :] = squashed
            own[k, pl.ds(r * tiles, tiles), :] = squashed.astype(BF16)
            shifted = ys[pl.ds(r * pitch + 7, tiles), :]
            before[k, pl.ds(r * tiles, tiles), :] = shifted.astype(BF16)

        @pl.when(k == 0)
        def _():
            pl.semaphore_wait(barrier, 1 + (width > 1) + has_down.astype(jnp.int32) + has_up.astype(jnp.int32))

        for at in range(parts):
            @pl.when(k == at)
            def _():
                gathered[at][me] = own[at]
                if width > 1:
                    copy(me, at, ACROSS, across).start()

                @pl.when(has_down)
                def _():
                    copy(me, at, DOWN, down).start()

                @pl.when(has_up)
                def _():
                    copy(me, at, UP, up).start()

                copy(me, at, SIB, sibling).start()
                if at >= 2 and depth > 1:
                    round_part(jnp.int32(1), at - 2)

        return carry

    paired = width > 1 and depth % 2 == 0
    mate = z + 1 - 2 * (z % 2)

    def late(k):
        return paired and 4 * k >= 3 * parts and parts > 1

    def along(z_of, way, target, onward, k):
        block = z_of * 2 * width + y * 2 + core
        landed(block, k)

        @pl.when(onward)
        def _():
            copy(block, k, way, target).start()

        if width > 1:
            @pl.when(jnp.logical_not(late(k) & (z_of == mate)))
            def _():
                copy(block, k, ACROSS, across).start()

        copy(block, k, SIB, sibling).start()

    def from_across(z_of, k):
        block = z_of * 2 * width + (1 - y) * 2 + core
        landed(block, k)
        if late(k):
            @pl.when((z_of == z) & (mate > z))
            def _():
                copy(block, k, UP, up).start()

            @pl.when((z_of == z) & (mate < z))
            def _():
                copy(block, k, DOWN, down).start()

        copy(block, k, SIB, sibling).start()

    def round_part(d, k):
        @pl.when(z - d >= 0)
        def _():
            along(z - d, UP, up, has_up, k)

        @pl.when(z + d < depth)
        def _():
            along(z + d, DOWN, down, has_down, k)

        if width > 1:
            @pl.when(z - d + 1 >= 0)
            def _():
                from_across(z - d + 1, k)

            @pl.when((d > 1) & (z + d - 1 < depth))
            def _():
                from_across(z + d - 1, k)

    def one_round(d, carry):
        for k in range(parts):
            round_part(d, k)
        return carry

    lax.fori_loop(0, parts, whiten_part, 0)

    if depth > 1:
        for k in range(max(parts - 2, 0), parts):
            round_part(jnp.int32(1), k)
        lax.fori_loop(2, depth, one_round, 0)

    partners = []
    mine = device[me]
    for m in range(matches):
        wanted = matchings[m, mine]
        partner = jnp.int32(0)
        for e in range(blocks):
            partner = jnp.where(device[e] == wanted, e, partner)
        partners.append(partner)

    def correlate_row(k, r, carry):
        span = pl.ds(pl.multiple_of(r * tiles, 16), tiles)
        left = jnp.concatenate([own[k, span, :], before[k, span, :]], axis=1)
        right = jnp.concatenate([gathered[k][partner, span, :] for partner in partners], axis=1)
        gram = lax.dot_general(left, right, (((0,), (0,)), ((), ())), preferred_element_type=F32)
        for m in range(matches):
            lanes = slice(m * LAGS, (m + 1) * LAGS)
            chosen = jnp.where(upper, gram[:LAGS, lanes], gram[LAGS:, lanes])
            terms = [chosen[:8]]
            for g in range(8, LAGS, 8):
                terms.append(pltpu.roll(chosen[g:g + 8], LAGS - g, 1))
            while len(terms) > 1:
                terms = [a + b for a, b in zip(terms[::2], terms[1::2])]
            acc[pl.ds(pl.multiple_of((m * rows + k * part + r) * 8, 8), 8), :] = terms[0]
        return carry

    def finish(k):
        def one(pair, carry):
            landed(2 * pair + 1 - core, k)
            return carry

        lax.fori_loop(0, blocks // 2, one, 0)
        lax.fori_loop(0, part, functools.partial(correlate_row, k), 0, unroll=UNROLL)

    for k in range(parts):
        round_part(jnp.int32(depth), k)
        if k > 0:
            finish(k - 1)
    finish(parts - 1)

    scale = 1.0 / total ** 0.5
    for m in range(matches):
        lags = acc[pl.ds(m * rows * 8, rows, stride=8), :]
        for s in range(1, 8):
            lags += pltpu.roll(acc[pl.ds(m * rows * 8 + s, rows, stride=8), :], LAGS - s, 1)
        out_ref[m] = lags * scale

    def sent(block, carry):
        b_core = block % 2
        b_y = (block // 2) % width
        b_z = block // (2 * width)
        straight = (b_core == core) & (b_y == y)
        for k in range(parts):
            @pl.when(b_core == core)
            def _():
                copy(block, k, SIB, sibling).wait_send()

            turned = jnp.bool_(False)
            if late(k):
                turned = (b_core == core) & (b_y != y) & (b_z == z)
            if width > 1:
                @pl.when(straight & jnp.logical_not(late(k) & (b_z == mate)))
                def _():
                    copy(block, k, ACROSS, across).wait_send()

            @pl.when((straight & has_up & (b_z <= z)) | (turned & (mate > z)))
            def _():
                copy(block, k, UP, up).wait_send()

            @pl.when((straight & has_down & (b_z >= z)) | (turned & (mate < z)))
            def _():
                copy(block, k, DOWN, down).wait_send()

        return carry

    lax.fori_loop(0, blocks, sent, 0)


def per_device(width, noise_window, fir_taps, matchings, block_device):
    rows, total = noise_window.shape
    matches, blocks = matchings.shape
    tiles = total // LAGS
    part = 8 if rows % 8 == 0 else rows
    parts = rows // part
    return pl.pallas_call(
        functools.partial(kernel, width, part),
        out_shape=jax.ShapeDtypeStruct((matches, rows, LAGS), F32),
        in_specs=[pl.BlockSpec(memory_space=pltpu.HBM)] * 4,
        out_specs=pl.BlockSpec(memory_space=pltpu.VMEM),
        scratch_shapes=[
            pltpu.VMEM((rows, total), F32),
            pltpu.VMEM(fir_taps.shape, F32),
            pltpu.SMEM(matchings.shape, jnp.int32),
            pltpu.SMEM(block_device.shape, jnp.int32),
            pltpu.VMEM((part * (tiles + 8), LAGS), F32),
            pltpu.VMEM((part * (tiles + 8), LAGS), F32),
            pltpu.VMEM((parts, part * tiles, LAGS), BF16),
            pltpu.VMEM((parts, part * tiles, LAGS), BF16),
            pltpu.VMEM((matches * rows * 8, LAGS), F32),
            pltpu.SemaphoreType.DMA((3 + parts,)),
            pltpu.SemaphoreType.DMA((4, blocks, parts)),
            pltpu.SemaphoreType.DMA((blocks, parts)),
        ] + [pltpu.VMEM((blocks, part * tiles, LAGS), BF16)] * parts,
        compiler_params=pltpu.CompilerParams(
            collective_id=0, has_side_effects=True, vmem_limit_bytes=48 * 2**20
        ),
    )(noise_window, fir_taps, matchings, block_device)


def plane_width(mesh):
    line = mesh.devices.reshape(mesh.shape["grp"], -1)[0]
    places = [getattr(d, "coords", None) for d in line]
    if any(p is None for p in places):
        return 1
    width = len({tuple(p[:2]) for p in places})
    return width if width == 2 and len(places) % 4 == 0 else 1


def solution(mesh):
    return jax.shard_map(
        functools.partial(per_device, plane_width(mesh)),
        mesh=mesh,
        in_specs=(P(("grp", "sta"), None), P(("grp", "sta"), None), P(), P()),
        out_specs=P(None, ("grp", "sta"), None),
        check_vma=False,
    )
```
